32 devices in a mesh: groups: 2 (over y), tm: 8 (over z, x), chan: 2 (over core).
Axes of the slice: x: 2, y: 2, z: 4, core: 2. Of those that a mesh axis runs over, the one named last changes fastest.
Arguments:
- series: bfloat16 [24576, 512], P(('groups', 'tm'), 'chan'), parts along dimension 0, may hold values from -6 to 6
- cotangent: bfloat16 [24576, 512], P(('groups', 'tm'), 'chan'), parts along dimension 0, may hold values from -3 to 3
- mode_index: int32 [1024], replicated, may hold values from 0 to 6143, as said below
- mix_weight: bfloat16 [2, 1024, 64, 512], P(None, 'tm', None, 'chan'), may hold values from -0.5 to 0.5
Outputs:
- activated: bfloat16 [24576, 512], P(('groups', 'tm'), 'chan'), parts along dimension 0
- series_grad: bfloat16 [24576, 512], P(('groups', 'tm'), 'chan'), parts along dimension 0
- weight_grad: float32 [4, 1024, 64, 512], P('groups', 'tm', None, 'chan'), parts along dimension 0
The draws below stay inside these ranges and needn't reach their ends.
There are 2 independent parts, one for each index of `groups`. The reference program is written for one: setup_inputs(seed, part) draws one part's arguments, and reference() takes and returns one part's arrays. A program takes and returns all parts, laid end to end along the dimension named above; an argument that names none is the same for every part. Nothing has to cross between parts.
Inputs may be any that keep to these rules, and one draw needn't show every extreme that they name: `mode_index`: the 1024 frequencies are distinct; 0 and 6143 are always among them.
All inputs are finite; a program needn't handle non-finite values.
Results may differ from the reference program's by a relative error of at most 0.0074.
Values may be sent and summed in bfloat16 or wider, within the bound.
A program may use at most 192 MiB of HBM per device.

```python
import math
import jax
import jax.numpy as jnp
from jax import lax

C = 512
M = 1024
BLK = 64
TIME_DEV = 1536
TIME = 12288


def draw_mode_index(key, part):
    key = jax.random.fold_in(key, 11)
    inner_modes = jax.random.permutation(key, TIME // 2 - 2)[:M - 2].astype(jnp.int32) + 1
    end_modes = jnp.array([0, TIME // 2 - 1], jnp.int32)
    chosen = jnp.concatenate([end_modes, inner_modes])
    shuffle = jax.random.permutation(jax.random.fold_in(key, 1), M)
    return chosen[shuffle]


def block_levels(rng, extent, cuts, smallest, high):
    def one(position, blocks):
        heights = jax.random.uniform(jax.random.fold_in(jax.random.fold_in(rng, 6), position), (blocks,), jnp.float32, smallest / len(cuts), high / len(cuts))
        return jnp.repeat(jnp.exp(heights), extent[position] // blocks).reshape((-1,) + (1,) * (len(extent) - position - 1))

    gain = one(*cuts[0])
    for cut in cuts[1:]:
        gain = gain * one(*cut)
    return gain


def noise(stream_key, shape, width, limit, shards=(), kind=jnp.bfloat16):
    values = width * jax.random.normal(stream_key, shape, jnp.float32)
    if shards:
        values = values * block_levels(stream_key, shape, shards, -0.22, 0.18)
    return jnp.clip(values, -limit, limit).astype(kind)


def setup_inputs(seed: int = 0, part: int = 0) -> dict:
    key_of = jax.random.split(jax.random.key(seed), 5)
    own_keys = jax.random.split(jax.random.fold_in(key_of[4], part), 5)
    series = noise(own_keys[0], (TIME, C), 1.0, 6.0, ((0, 8), (1, 2)))
    cotangent = noise(own_keys[1], (TIME, C), 0.5, 3.0, ((0, 8), (1, 2)))
    mode_index = draw_mode_index(jax.random.fold_in(key_of[4], 71), part)
    mix_weight = noise(key_of[3], (2, M, BLK, C), (2 * BLK) ** -0.5, 0.5, ((1, 8), (3, 2)))
    return {"series": series, "cotangent": cotangent, "mode_index": mode_index, "mix_weight": mix_weight}


def phase_table(mode_index, first_step, row_count, time_total):
    time_steps = first_step + jnp.arange(row_count, dtype=jnp.int32)
    high_part = (time_steps // 1024)[:, None]
    low_part = (time_steps % 1024)[:, None]
    frequency = mode_index[None, :]
    low_term = frequency * low_part % time_total
    high_term = frequency * high_part % time_total * 1024 % time_total
    residue = (low_term + high_term) % time_total
    phase_angle = residue.astype(jnp.float32) * (2.0 * math.pi / time_total)
    return (jnp.cos(phase_angle).astype(jnp.bfloat16), jnp.sin(phase_angle).astype(jnp.bfloat16))

def transform(signal, cos_table, sin_table, factor):
    dims = (((0,), (0,)), ((), ()))
    real_part = lax.dot_general(cos_table, signal, dims, preferred_element_type=jnp.float32)
    imag_part = lax.dot_general(sin_table, signal, dims, preferred_element_type=jnp.float32)
    return jnp.stack([real_part * factor, -imag_part * factor], axis=1)

def combine(spectrum, cos_table, sin_table, factor):
    first_dot = jnp.dot(cos_table, spectrum[:, 0], preferred_element_type=jnp.float32)
    second_dot = jnp.dot(sin_table, spectrum[:, 1], preferred_element_type=jnp.float32)
    return factor * (first_dot - second_dot)

def activate(pre_act):
    return jax.nn.gelu(pre_act, approximate=True)

def split_parts(spectrum, block_size):
    mode_rows, _, chan_width = spectrum.shape
    block_count = chan_width // block_size
    real_part = spectrum[:, 0].astype(jnp.float32).reshape(mode_rows, block_count, block_size)
    imag_part = spectrum[:, 1].astype(jnp.float32).reshape(mode_rows, block_count, block_size)
    return (real_part, imag_part)

def split_weight(weight):
    mode_rows, block_size, chan_width = (weight.shape[1], weight.shape[2], weight.shape[3])
    block_count = chan_width // block_size
    weight_real = weight[0].astype(jnp.float32).reshape(mode_rows, block_size, block_count, block_size)
    weight_imag = weight[1].astype(jnp.float32).reshape(mode_rows, block_size, block_count, block_size)
    return (weight_real, weight_imag)

def mix(spectrum, weight):
    mode_rows, _, chan_width = spectrum.shape
    real_part, imag_part = split_parts(spectrum, weight.shape[2])
    weight_real, weight_imag = split_weight(weight)
    out_real = jnp.einsum('mbi,mibj->mbj', real_part, weight_real) - jnp.einsum('mbi,mibj->mbj', imag_part, weight_imag)
    out_imag = jnp.einsum('mbi,mibj->mbj', real_part, weight_imag) + jnp.einsum('mbi,mibj->mbj', imag_part, weight_real)
    return jnp.stack([out_real.reshape(mode_rows, chan_width), out_imag.reshape(mode_rows, chan_width)], axis=1).astype(jnp.bfloat16)

def mix_grads(spectrum, weight, grad_spec):
    mode_rows, _, chan_width = spectrum.shape
    block_size = weight.shape[2]
    real_part, imag_part = split_parts(spectrum, block_size)
    grad_real, grad_imag = split_parts(grad_spec, block_size)
    weight_real, weight_imag = split_weight(weight)
    dw_real = jnp.einsum('mbi,mbj->mibj', real_part, grad_real) + jnp.einsum('mbi,mbj->mibj', imag_part, grad_imag)
    dw_imag = jnp.einsum('mbi,mbj->mibj', real_part, grad_imag) - jnp.einsum('mbi,mbj->mibj', imag_part, grad_real)
    weight_grad = jnp.stack([dw_real.reshape(mode_rows, block_size, chan_width), dw_imag.reshape(mode_rows, block_size, chan_width)], axis=0)
    dx_real = jnp.einsum('mibj,mbj->mbi', weight_real, grad_real) + jnp.einsum('mibj,mbj->mbi', weight_imag, grad_imag)
    dx_imag = jnp.einsum('mibj,mbj->mbi', weight_real, grad_imag) - jnp.einsum('mibj,mbj->mbi', weight_imag, grad_real)
    grad_spectrum = jnp.stack([dx_real.reshape(mode_rows, chan_width), dx_imag.reshape(mode_rows, chan_width)], axis=1).astype(jnp.bfloat16)
    return (weight_grad, grad_spectrum)

def reference(series, cotangent, mode_index, mix_weight):
    blocks = TIME // TIME_DEV
    scale_in = 1.0 / math.sqrt(TIME)
    scale_out = math.sqrt(2.0 / M)
    block_ids = jnp.arange(blocks, dtype=jnp.int32)
    series_blocks = series.reshape(blocks, TIME_DEV, C)
    cot_blocks = cotangent.reshape(blocks, TIME_DEV, C)

    def forward_step(running, block_item):
        block_index, signal = block_item
        cos_table, sin_table = phase_table(mode_index, block_index * TIME_DEV, TIME_DEV, TIME)
        return (running + transform(signal, cos_table, sin_table, scale_in), None)
    spectrum, _ = lax.scan(forward_step, jnp.zeros((M, 2, C), jnp.float32), (block_ids, series_blocks))
    spectrum_low = spectrum.astype(jnp.bfloat16)
    mixed = mix(spectrum_low, mix_weight)

    def middle_step(running, block_item):
        block_index, signal, cot_block = block_item
        cos_table, sin_table = phase_table(mode_index, block_index * TIME_DEV, TIME_DEV, TIME)
        pre_act = signal.astype(jnp.float32) + combine(mixed, cos_table, sin_table, scale_out)
        activated, pullback = jax.vjp(activate, pre_act)
        grad_pre = pullback(cot_block.astype(jnp.float32))[0]
        grad_low = grad_pre.astype(jnp.bfloat16)
        running = running + transform(grad_low, cos_table, sin_table, scale_out)
        return (running, (activated.astype(jnp.bfloat16), grad_pre))
    grad_mixed, (act_blocks, grad_blocks) = lax.scan(middle_step, jnp.zeros((M, 2, C), jnp.float32), (block_ids, series_blocks, cot_blocks))
    grad_mixed_low = grad_mixed.astype(jnp.bfloat16)
    weight_grad, grad_spectrum = mix_grads(spectrum_low, mix_weight, grad_mixed_low)

    def last_step(running, block_item):
        block_index, grad_pre = block_item
        cos_table, sin_table = phase_table(mode_index, block_index * TIME_DEV, TIME_DEV, TIME)
        result = grad_pre + combine(grad_spectrum, cos_table, sin_table, scale_in)
        return (running, result.astype(jnp.bfloat16))
    _, grad_series = lax.scan(last_step, jnp.zeros((), jnp.float32), (block_ids, grad_blocks))
    activated = act_blocks.reshape(TIME, C)
    series_grad = grad_series.reshape(TIME, C)
    return (activated, series_grad, weight_grad)
```

```python
import functools
import math

import jax
import jax.numpy as jnp
from jax import lax
from jax.experimental import pallas as pl
from jax.experimental.pallas import tpu as pltpu
from jax.sharding import PartitionSpec as P

LANES = 128
FINE = 16
MODES_PER_STEP = 8
VMEM_BYTES = 56 * 1024 * 1024
F32 = jnp.float32
BF16 = jnp.bfloat16


def base_tables(mode_index, first_step, device_count, time_total):
    owned = mode_index.shape[0] // device_count
    frequency = mode_index.reshape(device_count, 1, owned)
    frequency = jnp.broadcast_to(frequency, (device_count, 2, owned)).reshape(1, -1)
    quarter = jnp.arange(2, dtype=jnp.int32).reshape(1, 2, 1) * (time_total // 4)
    quarter = jnp.broadcast_to(quarter, (device_count, 2, owned)).reshape(1, -1)
    row = jnp.arange(32, dtype=jnp.int32)
    steps = jnp.where(row < FINE, row, (row - FINE) * FINE)
    steps = jnp.where(row == 24, first_step, steps)
    steps = jnp.where(row == 25, first_step + LANES, steps)
    steps = jnp.where(row == 26, LANES, steps)
    steps = jnp.where(row > 26, 0, steps)[:, None]
    low_term = frequency * (steps % 1024) % time_total
    high_term = frequency * (steps // 1024) % time_total * 1024 % time_total
    shift = jnp.where((row[:, None] == 24) | (row[:, None] == 25), quarter, 0)
    residue = (low_term + high_term + shift) % time_total
    angle = residue.astype(F32) * (2.0 * math.pi / time_total)
    return jnp.cos(angle), jnp.sin(angle)


def start_blocks(cos_ref, sin_ref, lanes):
    fine_cos, fine_sin = cos_ref[0:FINE, lanes], sin_ref[0:FINE, lanes]
    first, second = [], []
    for coarse in range(FINE, FINE + LANES // FINE):
        coarse_cos, coarse_sin = cos_ref[coarse : coarse + 1, lanes], sin_ref[coarse : coarse + 1, lanes]
        step_cos = coarse_cos * fine_cos - coarse_sin * fine_sin
        step_sin = coarse_sin * fine_cos + coarse_cos * fine_sin
        first.append(cos_ref[24:25, lanes] * step_cos - sin_ref[24:25, lanes] * step_sin)
        second.append(cos_ref[25:26, lanes] * step_cos - sin_ref[25:26, lanes] * step_sin)
    turn = 2.0 * cos_ref[26:27, lanes]
    turn = jnp.broadcast_to(turn, (LANES, LANES))
    return jnp.concatenate(first, axis=0), jnp.concatenate(second, axis=0), turn


def lane_block(index):
    return pl.ds(pl.multiple_of(index * LANES, LANES), LANES)


def fill_tables(cos_ref, sin_ref, table, table_t):
    step_blocks = (table if table is not None else table_t).shape[0 if table is not None else 1] // LANES

    def chunk(index, carry):
        lanes = lane_block(index)
        before, now, turn = start_blocks(cos_ref, sin_ref, lanes)
        if table is None:
            before, now, turn = before.T, now.T, turn.T
        for block in range(step_blocks):
            place = slice(block * LANES, (block + 1) * LANES)
            if table is None:
                table_t[lanes, place] = before.astype(BF16)
            else:
                table[place, lanes] = before.astype(BF16)
            before, now = now, turn * now - before
        return carry

    lax.fori_loop(0, cos_ref.shape[1] // LANES, chunk, 0)


def block_masks(block_size, width):
    row = lax.broadcasted_iota(jnp.int32, (block_size, width), 0)
    column = lax.broadcasted_iota(jnp.int32, (block_size, width), 1)
    pick = column % block_size == row
    left = lax.broadcasted_iota(jnp.int32, (width, width), 0) // block_size
    right = lax.broadcasted_iota(jnp.int32, (width, width), 1) // block_size
    return pick, (left == right).astype(F32).astype(BF16)


def spread_rows(ref, first_row, block_size):
    rows = [
        jnp.broadcast_to(ref[pl.ds(first_row + k, 1), :], (block_size, ref.shape[1]))
        for k in range(MODES_PER_STEP)
    ]
    return jnp.concatenate(rows, axis=0)


def expand(ref, first_row, pick, same_block):
    rows = spread_rows(ref, first_row, pick.shape[0])
    rows = jnp.where(jnp.concatenate([pick] * MODES_PER_STEP, axis=0), rows, 0.0).astype(BF16)
    return jnp.dot(rows, same_block, preferred_element_type=F32)


def fold(values, block_size):
    return values.reshape(MODES_PER_STEP, block_size, values.shape[1]).sum(axis=1)


def mode_weights(weight, part, first_row):
    rows = weight[part, pl.ds(first_row, MODES_PER_STEP)]
    return rows.reshape(rows.shape[0] * rows.shape[1], rows.shape[2]).astype(F32)


def spectral_kernel(
    scale_in,
    scale_out,
    count,
    cos_ref,
    sin_ref,
    series,
    cotangent,
    weight_hbm,
    activated,
    series_grad,
    spectrum_out,
    grad_out,
    weight,
    table,
    table_t,
    field,
    grad_pre,
    grad_low,
    partial,
    pair_in,
    pair_sum,
    line_in,
    gathered,
    spectrum,
    rows_out,
    weight_sem,
    pair_send,
    pair_recv,
    line_send,
    line_recv,
    share_send,
    share_recv,
    cross_send,
    cross_recv,
):
    half = count // 2
    owned = weight.shape[1]
    block_size = weight.shape[2]
    rows = 2 * owned
    time_rows, width = series.shape
    me = lax.axis_index("tm")
    high, low = me // 2, me % 2
    partner = high * 2 + 1 - low

    def peer(offset):
        return lax.rem(high + offset, half) * 2 + low

    def block(device):
        return pl.ds(pl.multiple_of(device * rows, rows), rows)

    def copy(source, target, send_sem, recv_sem, device):
        return pltpu.make_async_remote_copy(
            src_ref=source,
            dst_ref=target,
            send_sem=send_sem,
            recv_sem=recv_sem,
            device_id={"tm": device},
            device_id_type=pl.DeviceIdType.MESH,
        )

    load = pltpu.make_async_copy(weight_hbm, weight, weight_sem)
    load.start()
    barrier = pltpu.get_barrier_semaphore()
    pl.semaphore_signal(barrier, inc=1, device_id={"tm": partner}, device_id_type=pl.DeviceIdType.MESH)

    def greet(offset, carry):
        pl.semaphore_signal(barrier, inc=1, device_id={"tm": peer(offset)}, device_id_type=pl.DeviceIdType.MESH)
        return carry

    lax.fori_loop(1, half, greet, 0)

    def reduce_scatter(phase, signal, factor, meanwhile):
        def pair_copy(k):
            target = lax.rem(high + 1 + k, half) * 2 + 1 - low
            return copy(
                partial.at[phase, block(target)],
                pair_in.at[phase, k],
                pair_send.at[phase, k],
                pair_recv.at[phase, k],
                partner,
            )

        def line_copy(k):
            return copy(
                pair_sum.at[phase, k],
                line_in.at[phase, k],
                line_send.at[phase, k],
                line_recv.at[phase, k],
                peer(k + 1),
            )

        def project(device):
            product = jnp.dot(table_t[block(device), :], signal[...], preferred_element_type=F32)
            partial[phase, block(device), :] = (product * factor).astype(BF16)

        def send_pair(k, carry):
            project(lax.rem(high + 1 + k, half) * 2 + 1 - low)
            pair_copy(k).start()
            return carry

        lax.fori_loop(0, half, send_pair, 0)

        def own_part(k, carry):
            project(peer(k + 1))
            return carry

        lax.fori_loop(0, half, own_part, 0)

        def send_line(k, carry):
            pair_copy(k).wait_recv()
            own = partial[phase, block(peer(k + 1)), :].astype(F32)
            pair_sum[phase, k] = (own + pair_in[phase, k].astype(F32)).astype(BF16)
            line_copy(k).start()
            return carry

        lax.fori_loop(0, half - 1, send_line, 0)
        meanwhile()
        pair_copy(half - 1).wait_recv()
        total = partial[phase, block(me), :].astype(F32) + pair_in[phase, half - 1].astype(F32)

        def add(k, total):
            line_copy(k).wait_recv()
            return total + line_in[phase, k].astype(F32)

        for k in range(half - 1) if half <= 8 else ():
            total = add(k, total)
        if half > 8:
            total = lax.fori_loop(0, half - 1, add, total)
        spectrum[phase] = total.astype(BF16).astype(F32)

        def done(k, carry):
            pair_copy(k).wait_send()
            return carry

        lax.fori_loop(0, half, done, 0)

        def done_line(k, carry):
            line_copy(k).wait_send()
            return carry

        lax.fori_loop(0, half - 1, done_line, 0)

    def add_block(phase, first_row, depth, begin):
        place = pl.ds(pl.multiple_of(first_row, depth), depth)
        right = gathered[phase, place, :]

        def tile(t, carry):
            steps = pl.ds(pl.multiple_of(t * 2 * LANES, 2 * LANES), 2 * LANES)
            product = jnp.dot(table[steps, place], right, preferred_element_type=F32)
            if begin:
                field[steps, :] = product
            else:
                field[steps, :] += product
            return carry

        lax.fori_loop(0, time_rows // (2 * LANES), tile, 0)

    def gather(phase):
        early = rows % LANES == 0

        def share_copy(k):
            return copy(
                gathered.at[phase, block(me)],
                gathered.at[phase, block(me)],
                share_send.at[phase, k],
                share_recv.at[phase, k],
                peer(k),
            )

        def cross_copy(k):
            held = block(lax.rem(high - k + half, half) * 2 + low)
            return copy(
                gathered.at[phase, held],
                gathered.at[phase, held],
                cross_send.at[phase, k],
                cross_recv.at[phase, k],
                partner,
            )

        def arrival(device, recv_sem):
            place = gathered.at[phase, block(device)]
            return copy(place, place, recv_sem, recv_sem, partner)

        gathered[phase, block(me), :] = rows_out[...].astype(BF16)
        cross_copy(0).start()

        def share(k, carry):
            share_copy(k).start()
            return carry

        lax.fori_loop(1, half, share, 0)
        if early:
            add_block(phase, me * rows, rows, True)

        def forward(k, carry):
            device = lax.rem(high - k + half, half) * 2 + low
            arrival(device, share_recv.at[phase, k]).wait_recv()
            cross_copy(k).start()
            if early:
                add_block(phase, device * rows, rows, False)
            return carry

        lax.fori_loop(1, half, forward, 0)

        def receive(k, carry):
            device = lax.rem(high - k + half, half) * 2 + 1 - low
            arrival(device, cross_recv.at[phase, k]).wait_recv()
            if early:
                add_block(phase, device * rows, rows, False)
            return carry

        lax.fori_loop(0, half, receive, 0)
        if not early:
            depth = 2 * LANES
            add_block(phase, 0, depth, True)

            def rest(unit, carry):
                add_block(phase, unit * depth, depth, False)
                return carry

            lax.fori_loop(1, count * rows // depth, rest, 0)

        def done(k, carry):
            share_copy(k).wait_send()
            cross_copy(k).wait_send()
            return carry

        lax.fori_loop(1, half, done, 0)
        cross_copy(0).wait_send()

    pick, same_block = block_masks(block_size, width)

    def mix(step, carry):
        first = pl.multiple_of(step * MODES_PER_STEP, MODES_PER_STEP)
        second = pl.multiple_of(owned + step * MODES_PER_STEP, MODES_PER_STEP)
        x_real = expand(spectrum.at[0], first, pick, same_block)
        x_imag = expand(spectrum.at[0], second, pick, same_block)
        w_real, w_imag = mode_weights(weight, 0, first), mode_weights(weight, 1, first)
        rows_out[pl.ds(first, MODES_PER_STEP), :] = fold(x_real * w_real - x_imag * w_imag, block_size)
        rows_out[pl.ds(second, MODES_PER_STEP), :] = fold(x_real * w_imag + x_imag * w_real, block_size)
        return carry

    def mix_back(step, carry):
        first = pl.multiple_of(step * MODES_PER_STEP, MODES_PER_STEP)
        second = pl.multiple_of(owned + step * MODES_PER_STEP, MODES_PER_STEP)
        g_real = spread_rows(spectrum.at[1], first, block_size)
        g_imag = spread_rows(spectrum.at[1], second, block_size)
        w_real, w_imag = mode_weights(weight, 0, first), mode_weights(weight, 1, first)
        chosen = jnp.concatenate([pick] * MODES_PER_STEP, axis=0)

        def gathered_rows(values):
            sums = jnp.dot(values.astype(BF16), same_block, preferred_element_type=F32)
            return fold(jnp.where(chosen, sums, 0.0), block_size)

        rows_out[pl.ds(first, MODES_PER_STEP), :] = gathered_rows(w_real * g_real + w_imag * g_imag)
        rows_out[pl.ds(second, MODES_PER_STEP), :] = gathered_rows(w_real * g_imag - w_imag * g_real)
        return carry

    fill_tables(cos_ref, sin_ref, None, table_t)
    pl.semaphore_wait(barrier, half)
    reduce_scatter(0, series, scale_in, lambda: fill_tables(cos_ref, sin_ref, table, None))
    load.wait()
    lax.fori_loop(0, owned // MODES_PER_STEP, mix, 0)
    gather(0)

    slope = math.sqrt(2.0 / math.pi)

    def activate(t, carry):
        steps = pl.ds(pl.multiple_of(t * LANES, LANES), LANES)
        value = series[steps, :].astype(F32) + scale_out * field[steps, :]
        square = value * value
        tanh = jnp.tanh(slope * (value + 0.044715 * (square * value)))
        gate = 0.5 * (1.0 + tanh)
        activated[steps, :] = (value * gate).astype(BF16)
        inner = slope * (1.0 + 3.0 * 0.044715 * square)
        derivative = gate + 0.5 * value * (1.0 - tanh * tanh) * inner
        grad = cotangent[steps, :].astype(F32) * derivative
        grad_pre[steps, :] = grad
        grad_low[steps, :] = grad.astype(BF16)
        return carry

    lax.fori_loop(0, time_rows // LANES, activate, 0)
    reduce_scatter(1, grad_low, scale_out, lambda: None)
    lax.fori_loop(0, owned // MODES_PER_STEP, mix_back, 0)
    spectrum_out[...] = spectrum[0]
    grad_out[...] = spectrum[1]
    gather(1)

    def finish(t, carry):
        steps = pl.ds(pl.multiple_of(t * LANES, LANES), LANES)
        series_grad[steps, :] = (grad_pre[steps, :] + scale_in * field[steps, :]).astype(BF16)
        return carry

    lax.fori_loop(0, time_rows // LANES, finish, 0)


def weight_grad_kernel(x_real, x_imag, g_real, g_imag, out):
    block_size, width = out.shape[2], out.shape[3]
    pick, same_block = block_masks(block_size, width)
    shape = (MODES_PER_STEP, block_size, width)
    xr, xi = expand(x_real, 0, pick, same_block), expand(x_imag, 0, pick, same_block)
    gr, gi = spread_rows(g_real, 0, block_size), spread_rows(g_imag, 0, block_size)
    out[0] = (xr * gr + xi * gi).reshape(shape)
    out[1] = (xr * gi - xi * gr).reshape(shape)


def weight_gradient(spectrum, grad, block_size):
    owned, width = spectrum.shape[0] // 2, spectrum.shape[1]
    steps = owned // MODES_PER_STEP
    real = pl.BlockSpec((MODES_PER_STEP, width), lambda g: (g, 0))
    imag = pl.BlockSpec((MODES_PER_STEP, width), lambda g: (g + steps, 0))
    return pl.pallas_call(
        weight_grad_kernel,
        grid=(steps,),
        in_specs=[real, imag, real, imag],
        out_specs=pl.BlockSpec((2, MODES_PER_STEP, block_size, width), lambda g: (0, g, 0, 0)),
        out_shape=jax.ShapeDtypeStruct((2, owned, block_size, width), F32),
        compiler_params=pltpu.CompilerParams(vmem_limit_bytes=VMEM_BYTES),
    )(spectrum, spectrum, grad, grad)


def body(series, cotangent, mode_index, mix_weight):
    time_rows, width = series.shape
    count = lax.axis_size("tm")
    modes = mode_index.shape[0]
    owned = mix_weight.shape[1]
    rows = 2 * owned
    half = count // 2
    time_total = time_rows * count
    cos_base, sin_base = base_tables(mode_index, lax.axis_index("tm") * time_rows, count, time_total)
    kernel = functools.partial(
        spectral_kernel, 1.0 / math.sqrt(time_total), math.sqrt(2.0 / modes), count
    )
    vmem = pl.BlockSpec(memory_space=pltpu.VMEM)
    sems = pltpu.SemaphoreType.DMA((2, half))
    activated, series_grad, spectrum, grad = pl.pallas_call(
        kernel,
        in_specs=[vmem] * 4 + [pl.BlockSpec(memory_space=pl.ANY)],
        out_specs=[vmem] * 4,
        out_shape=[
            jax.ShapeDtypeStruct((time_rows, width), BF16),
            jax.ShapeDtypeStruct((time_rows, width), BF16),
            jax.ShapeDtypeStruct((rows, width), F32),
            jax.ShapeDtypeStruct((rows, width), F32),
        ],
        scratch_shapes=[
            pltpu.VMEM(mix_weight.shape, BF16),
            pltpu.VMEM((time_rows, 2 * modes), BF16),
            pltpu.VMEM((2 * modes, time_rows), BF16),
            pltpu.VMEM((time_rows, width), F32),
            pltpu.VMEM((time_rows, width), F32),
            pltpu.VMEM((time_rows, width), BF16),
            pltpu.VMEM((2, 2 * modes, width), BF16),
            pltpu.VMEM((2, half, rows, width), BF16),
            pltpu.VMEM((2, half, rows, width), BF16),
            pltpu.VMEM((2, half, rows, width), BF16),
            pltpu.VMEM((2, 2 * modes, width), BF16),
            pltpu.VMEM((2, rows, width), F32),
            pltpu.VMEM((rows, width), F32),
            pltpu.SemaphoreType.DMA,
        ]
        + [sems] * 8,
        compiler_params=pltpu.CompilerParams(
            collective_id=0, has_side_effects=True, vmem_limit_bytes=VMEM_BYTES
        ),
    )(cos_base, sin_base, series, cotangent, mix_weight)
    return activated, series_grad, weight_gradient(spectrum, grad, mix_weight.shape[2])


def solution(mesh):
    in_specs = (
        P(("groups", "tm"), "chan"),
        P(("groups", "tm"), "chan"),
        P(),
        P(None, "tm", None, "chan"),
    )
    out_specs = (
        P(("groups", "tm"), "chan"),
        P(("groups", "tm"), "chan"),
        P("groups", "tm", None, "chan"),
    )
    return jax.shard_map(body, mesh=mesh, in_specs=in_specs, out_specs=out_specs, check_vma=False)
```

```python
import functools
import math

import jax
import jax.numpy as jnp
from jax import lax
from jax.experimental import pallas as pl
from jax.experimental.pallas import tpu as pltpu
from jax.sharding import PartitionSpec as P

LANES = 128
FINE = 16
PIECE_MODES = 64
MODES_PER_STEP = 8
VMEM_BYTES = 56 * 1024 * 1024
F32 = jnp.float32
BF16 = jnp.bfloat16


def base_tables(mode_index, first_step, device_count, time_total):
    owned = mode_index.shape[0] // device_count
    depth = min(owned, PIECE_MODES)
    frequency = mode_index.reshape(-1, 1, depth)
    shape = (frequency.shape[0], 2, depth)
    frequency = jnp.broadcast_to(frequency, shape).reshape(1, -1)
    quarter = jnp.arange(2, dtype=jnp.int32).reshape(1, 2, 1) * (time_total // 4)
    quarter = jnp.broadcast_to(quarter, shape).reshape(1, -1)
    row = jnp.arange(32, dtype=jnp.int32)
    steps = jnp.where(row < FINE, row, (row - FINE) * FINE)
    steps = jnp.where(row == 24, first_step, steps)
    steps = jnp.where(row == 25, first_step + LANES, steps)
    steps = jnp.where(row == 26, LANES, steps)
    steps = jnp.where(row > 26, 0, steps)[:, None]
    low_term = frequency * (steps % 1024) % time_total
    high_term = frequency * (steps // 1024) % time_total * 1024 % time_total
    shift = jnp.where((row[:, None] == 24) | (row[:, None] == 25), quarter, 0)
    residue = (low_term + high_term + shift) % time_total
    angle = residue.astype(F32) * (2.0 * math.pi / time_total)
    return jnp.cos(angle), jnp.sin(angle)


def start_blocks(cos_ref, sin_ref, lanes):
    fine_cos, fine_sin = cos_ref[0:FINE, lanes], sin_ref[0:FINE, lanes]
    first, second = [], []
    for coarse in range(FINE, FINE + LANES // FINE):
        coarse_cos, coarse_sin = cos_ref[coarse : coarse + 1, lanes], sin_ref[coarse : coarse + 1, lanes]
        step_cos = coarse_cos * fine_cos - coarse_sin * fine_sin
        step_sin = coarse_sin * fine_cos + coarse_cos * fine_sin
        first.append(cos_ref[24:25, lanes] * step_cos - sin_ref[24:25, lanes] * step_sin)
        second.append(cos_ref[25:26, lanes] * step_cos - sin_ref[25:26, lanes] * step_sin)
    turn = 2.0 * cos_ref[26:27, lanes]
    turn = jnp.broadcast_to(turn, (LANES, LANES))
    return jnp.concatenate(first, axis=0), jnp.concatenate(second, axis=0), turn


def lane_block(index):
    return pl.ds(pl.multiple_of(index * LANES, LANES), LANES)


def fill_tables(cos_ref, sin_ref, table, table_t):
    step_blocks = (table if table is not None else table_t).shape[0 if table is not None else 1] // LANES

    def chunk(index, carry):
        lanes = lane_block(index)
        before, now, turn = start_blocks(cos_ref, sin_ref, lanes)
        if table is None:
            before, now, turn = before.T, now.T, turn.T
        for block in range(step_blocks):
            place = slice(block * LANES, (block + 1) * LANES)
            if table is None:
                table_t[lanes, place] = before.astype(BF16)
            else:
                table[place, lanes] = before.astype(BF16)
            before, now = now, turn * now - before
        return carry

    lax.fori_loop(0, cos_ref.shape[1] // LANES, chunk, 0)


def block_masks(block_size, width):
    row = lax.broadcasted_iota(jnp.int32, (block_size, width), 0)
    column = lax.broadcasted_iota(jnp.int32, (block_size, width), 1)
    pick = lax.rem(column, block_size) == row
    left = lax.div(lax.broadcasted_iota(jnp.int32, (width, width), 0), block_size)
    right = lax.div(lax.broadcasted_iota(jnp.int32, (width, width), 1), block_size)
    return pick, (left == right).astype(F32).astype(BF16)


def spread_rows(ref, first_row, block_size):
    rows = [
        jnp.broadcast_to(ref[pl.ds(first_row + k, 1), :], (block_size, ref.shape[1]))
        for k in range(MODES_PER_STEP)
    ]
    return jnp.concatenate(rows, axis=0)


def expand(ref, first_row, pick, same_block):
    rows = spread_rows(ref, first_row, pick.shape[0])
    rows = jnp.where(jnp.concatenate([pick] * MODES_PER_STEP, axis=0), rows, 0.0).astype(BF16)
    return jnp.dot(rows, same_block, preferred_element_type=F32)


def fold(values, block_size):
    return values.reshape(MODES_PER_STEP, block_size, values.shape[1]).sum(axis=1)


def loop(begin, end, step):
    if end - begin <= 8:
        for k in range(begin, end):
            step(k)
    else:

        def one(k, carry):
            step(k)
            return carry

        lax.fori_loop(begin, end, one, 0)


def mode_weights(weight, part, first_row):
    rows = weight[part, pl.ds(first_row, MODES_PER_STEP)]
    return rows.reshape(rows.shape[0] * rows.shape[1], rows.shape[2]).astype(F32)


def spectral_kernel(
    scale_in,
    scale_out,
    count,
    cos_ref,
    sin_ref,
    series,
    cotangent,
    weight_hbm,
    activated,
    series_grad,
    spectrum_out,
    grad_out,
    weight,
    table,
    table_t,
    field,
    grad_pre,
    grad_low,
    partial,
    pair_in,
    pair_sum,
    line_in,
    gathered,
    spectrum,
    rows_out,
    weight_sem,
    pair_send,
    pair_recv,
    line_send,
    line_recv,
    share_send,
    share_recv,
    cross_send,
    cross_recv,
):
    half = count // 2
    owned = weight.shape[1]
    block_size = weight.shape[2]
    rows = 2 * owned
    depth = min(owned, PIECE_MODES)
    pieces = owned // depth
    piece_rows = 2 * depth
    time_rows, width = series.shape
    me = lax.axis_index("tm")
    high, low = lax.div(me, 2), lax.rem(me, 2)
    partner = high * 2 + 1 - low

    def peer(offset):
        return lax.rem(high + offset, half) * 2 + low

    def offset_of(k):
        if half != 4:
            return k + 1
        return (2, 1, 3, 4)[k]

    def piece(device, q):
        return pl.ds(pl.multiple_of(device * rows + q * piece_rows, piece_rows), piece_rows)

    def block(device):
        return pl.ds(pl.multiple_of(device * rows, rows), rows)

    def copy(source, target, send_sem, recv_sem, device):
        return pltpu.make_async_remote_copy(
            src_ref=source,
            dst_ref=target,
            send_sem=send_sem,
            recv_sem=recv_sem,
            device_id={"tm": device},
            device_id_type=pl.DeviceIdType.MESH,
        )

    load = pltpu.make_async_copy(weight_hbm, weight, weight_sem)
    load.start()
    barrier = pltpu.get_barrier_semaphore()
    pl.semaphore_signal(barrier, inc=1, device_id={"tm": partner}, device_id_type=pl.DeviceIdType.MESH)

    def greet(offset, carry):
        pl.semaphore_signal(barrier, inc=1, device_id={"tm": peer(offset)}, device_id_type=pl.DeviceIdType.MESH)
        return carry

    lax.fori_loop(1, half, greet, 0)

    def pair_target(k):
        return lax.rem(high + offset_of(k), half) * 2 + 1 - low

    def pair_copy(phase, q, k):
        return copy(
            partial.at[phase, piece(pair_target(k), q)],
            pair_in.at[phase, q, k],
            pair_send.at[phase, q, k],
            pair_recv.at[phase, q, k],
            partner,
        )

    def line_copy(phase, q, k):
        return copy(
            pair_sum.at[phase, q, k],
            line_in.at[phase, q, k],
            line_send.at[phase, q, k],
            line_recv.at[phase, q, k],
            peer(offset_of(k)),
        )

    def share_copy(phase, q, k):
        mine = gathered.at[phase, piece(me, q)]
        return copy(mine, mine, share_send.at[phase, q, k], share_recv.at[phase, q, k], peer(k))

    def cross_copy(phase, q, k):
        held = gathered.at[phase, piece(lax.rem(high - k + half, half) * 2 + low, q)]
        return copy(held, held, cross_send.at[phase, q, k], cross_recv.at[phase, q, k], partner)

    def arrival(phase, device, q, recv_sem):
        place = gathered.at[phase, piece(device, q)]
        return copy(place, place, recv_sem, recv_sem, partner)

    def exchange(phase, signal, factor, mode_step, meanwhile):
        def project(device):
            product = jnp.dot(table_t[block(device), :], signal[...], preferred_element_type=F32)
            partial[phase, block(device), :] = (product * factor).astype(BF16)

        def send_first(k):
            project(pair_target(k))
            pair_copy(phase, 0, k).start()

        def forward(q):
            def one(k):
                device = lax.rem(high - k + half, half) * 2 + low
                arrival(phase, device, q, share_recv.at[phase, q, k]).wait_recv()
                cross_copy(phase, q, k).start()

            loop(1, half, one)

        def line_piece(q):
            def send_line(k):
                pair_copy(phase, q, k).wait_recv()
                own = partial[phase, piece(peer(offset_of(k)), q), :].astype(F32)
                pair_sum[phase, q, k] = (own + pair_in[phase, q, k].astype(F32)).astype(BF16)
                line_copy(phase, q, k).start()

            loop(0, half - 1, send_line)

        def mix_piece(q):
            place = pl.ds(q * piece_rows, piece_rows)
            pair_copy(phase, q, half - 1).wait_recv()
            spectrum[phase, place, :] = (
                partial[phase, piece(me, q), :].astype(F32) + pair_in[phase, q, half - 1].astype(F32)
            )

            def add(k):
                line_copy(phase, q, k).wait_recv()
                spectrum[phase, place, :] += line_in[phase, q, k].astype(F32)

            loop(0, half - 1, add)
            spectrum[phase, place, :] = spectrum[phase, place, :].astype(BF16).astype(F32)
            if phase == 0 and q == 0:
                load.wait()

            def mode_steps(step, carry):
                first = pl.multiple_of(q * piece_rows + step * MODES_PER_STEP, MODES_PER_STEP)
                mode_step(first, first + depth, pl.multiple_of(q * depth + step * MODES_PER_STEP, MODES_PER_STEP))
                return carry

            lax.fori_loop(0, depth // MODES_PER_STEP, mode_steps, 0)
            gathered[phase, piece(me, q), :] = rows_out[place, :].astype(BF16)
            loop(1, half, lambda k: share_copy(phase, q, k).start())
            cross_copy(phase, q, 0).start()

        loop(0, half, send_first)
        for q in range(1, pieces):
            loop(0, half, lambda k: pair_copy(phase, q, k).start())
        loop(0, half, lambda k: project(peer(offset_of(k))))
        for q in range(pieces):
            line_piece(q)
            if q == 0:
                meanwhile()
            if q > 0:
                mix_piece(q - 1)
            if q > 1:
                forward(q - 2)
        mix_piece(pieces - 1)
        if pieces > 1:
            forward(pieces - 2)
        early = rows % LANES == 0
        if early:
            add_block(phase, me * rows, rows, True)
        forward(pieces - 1)
        if early:
            loop(1, half, lambda k: add_block(phase, (lax.rem(high - k + half, half) * 2 + low) * rows, rows, False))

        def receive(k):
            device = lax.rem(high - k + half, half) * 2 + 1 - low
            for q in range(pieces):
                arrival(phase, device, q, cross_recv.at[phase, q, k]).wait_recv()
            if early:
                add_block(phase, device * rows, rows, False)

        loop(0, half, receive)
        if not early:
            add_block(phase, 0, 2 * LANES, True)
            loop(1, count * rows // (2 * LANES), lambda u: add_block(phase, u * 2 * LANES, 2 * LANES, False))

        def sent(k):
            for q in range(pieces):
                pair_copy(phase, q, k).wait_send()
                cross_copy(phase, q, k).wait_send()

        def sent_line(k):
            for q in range(pieces):
                line_copy(phase, q, k).wait_send()
                share_copy(phase, q, k + 1).wait_send()

        loop(0, half, sent)
        loop(0, half - 1, sent_line)

    def add_block(phase, first_row, depth, begin):
        place = pl.ds(pl.multiple_of(first_row, depth), depth)
        right = gathered[phase, place, :]

        def tile(t, carry):
            steps = pl.ds(pl.multiple_of(t * 2 * LANES, 2 * LANES), 2 * LANES)
            product = jnp.dot(table[steps, place], right, preferred_element_type=F32)
            if begin:
                field[steps, :] = product
            else:
                field[steps, :] += product
            return carry

        lax.fori_loop(0, time_rows // (2 * LANES), tile, 0)

    pick, same_block = block_masks(block_size, width)

    def mix(first, second, mode):
        x_real = expand(spectrum.at[0], first, pick, same_block)
        x_imag = expand(spectrum.at[0], second, pick, same_block)
        w_real, w_imag = mode_weights(weight, 0, mode), mode_weights(weight, 1, mode)
        rows_out[pl.ds(first, MODES_PER_STEP), :] = fold(x_real * w_real - x_imag * w_imag, block_size)
        rows_out[pl.ds(second, MODES_PER_STEP), :] = fold(x_real * w_imag + x_imag * w_real, block_size)

    def mix_back(first, second, mode):
        g_real = spread_rows(spectrum.at[1], first, block_size)
        g_imag = spread_rows(spectrum.at[1], second, block_size)
        w_real, w_imag = mode_weights(weight, 0, mode), mode_weights(weight, 1, mode)
        chosen = jnp.concatenate([pick] * MODES_PER_STEP, axis=0)

        def gathered_rows(values):
            sums = jnp.dot(values.astype(BF16), same_block, preferred_element_type=F32)
            return fold(jnp.where(chosen, sums, 0.0), block_size)

        rows_out[pl.ds(first, MODES_PER_STEP), :] = gathered_rows(w_real * g_real + w_imag * g_imag)
        rows_out[pl.ds(second, MODES_PER_STEP), :] = gathered_rows(w_real * g_imag - w_imag * g_real)

    fill_tables(cos_ref, sin_ref, None, table_t)
    pl.semaphore_wait(barrier, half)
    exchange(0, series, scale_in, mix, lambda: fill_tables(cos_ref, sin_ref, table, None))

    slope = math.sqrt(2.0 / math.pi)

    def activate(t, carry):
        steps = pl.ds(pl.multiple_of(t * LANES, LANES), LANES)
        value = series[steps, :].astype(F32) + scale_out * field[steps, :]
        square = value * value
        tanh = jnp.tanh(slope * (value + 0.044715 * (square * value)))
        gate = 0.5 * (1.0 + tanh)
        activated[steps, :] = (value * gate).astype(BF16)
        inner = slope * (1.0 + 3.0 * 0.044715 * square)
        derivative = gate + 0.5 * value * (1.0 - tanh * tanh) * inner
        grad = cotangent[steps, :].astype(F32) * derivative
        grad_pre[steps, :] = grad
        grad_low[steps, :] = grad.astype(BF16)
        return carry

    lax.fori_loop(0, time_rows // LANES, activate, 0)
    exchange(1, grad_low, scale_out, mix_back, lambda: None)
    spectrum_out[...] = spectrum[0]
    grad_out[...] = spectrum[1]

    def finish(t, carry):
        steps = pl.ds(pl.multiple_of(t * LANES, LANES), LANES)
        series_grad[steps, :] = (grad_pre[steps, :] + scale_in * field[steps, :]).astype(BF16)
        return carry

    lax.fori_loop(0, time_rows // LANES, finish, 0)


def weight_grad_kernel(x_real, x_imag, g_real, g_imag, out, pick_ref, same_ref):
    block_size, width = out.shape[2], out.shape[3]

    @pl.when(pl.program_id(0) == 0)
    def _():
        pick, same_block = block_masks(block_size, width)
        pick_ref[...] = pick.astype(F32)
        same_ref[...] = same_block

    pick, same_block = pick_ref[...] > 0.5, same_ref[...]
    shape = (MODES_PER_STEP, block_size, width)
    xr, xi = expand(x_real, 0, pick, same_block), expand(x_imag, 0, pick, same_block)
    gr, gi = spread_rows(g_real, 0, block_size), spread_rows(g_imag, 0, block_size)
    out[0] = (xr * gr + xi * gi).reshape(shape)
    out[1] = (xr * gi - xi * gr).reshape(shape)


def weight_gradient(spectrum, grad, block_size):
    owned, width = spectrum.shape[0] // 2, spectrum.shape[1]
    steps = owned // MODES_PER_STEP
    per_piece = min(owned, PIECE_MODES) // MODES_PER_STEP

    def place(part):
        return lambda g: (g // per_piece * (2 * per_piece) + part * per_piece + g % per_piece, 0)

    real = pl.BlockSpec((MODES_PER_STEP, width), place(0))
    imag = pl.BlockSpec((MODES_PER_STEP, width), place(1))
    return pl.pallas_call(
        weight_grad_kernel,
        grid=(steps,),
        in_specs=[real, imag, real, imag],
        out_specs=pl.BlockSpec((2, MODES_PER_STEP, block_size, width), lambda g: (0, g, 0, 0)),
        out_shape=jax.ShapeDtypeStruct((2, owned, block_size, width), F32),
        scratch_shapes=[pltpu.VMEM((block_size, width), F32), pltpu.VMEM((width, width), BF16)],
        compiler_params=pltpu.CompilerParams(vmem_limit_bytes=VMEM_BYTES),
    )(spectrum, spectrum, grad, grad)


def body(series, cotangent, mode_index, mix_weight):
    time_rows, width = series.shape
    count = lax.axis_size("tm")
    modes = mode_index.shape[0]
    owned = mix_weight.shape[1]
    rows = 2 * owned
    half = count // 2
    pieces = max(1, owned // PIECE_MODES)
    time_total = time_rows * count
    cos_base, sin_base = base_tables(mode_index, lax.axis_index("tm") * time_rows, count, time_total)
    kernel = functools.partial(
        spectral_kernel, 1.0 / math.sqrt(time_total), math.sqrt(2.0 / modes), count
    )
    vmem = pl.BlockSpec(memory_space=pltpu.VMEM)
    sems = pltpu.SemaphoreType.DMA((2, pieces, half))
    activated, series_grad, spectrum, grad = pl.pallas_call(
        kernel,
        in_specs=[vmem] * 4 + [pl.BlockSpec(memory_space=pl.ANY)],
        out_specs=[vmem] * 4,
        out_shape=[
            jax.ShapeDtypeStruct((time_rows, width), BF16),
            jax.ShapeDtypeStruct((time_rows, width), BF16),
            jax.ShapeDtypeStruct((rows, width), F32),
            jax.ShapeDtypeStruct((rows, width), F32),
        ],
        scratch_shapes=[
            pltpu.VMEM(mix_weight.shape, BF16),
            pltpu.VMEM((time_rows, 2 * modes), BF16),
            pltpu.VMEM((2 * modes, time_rows), BF16),
            pltpu.VMEM((time_rows, width), F32),
            pltpu.VMEM((time_rows, width), F32),
            pltpu.VMEM((time_rows, width), BF16),
            pltpu.VMEM((2, 2 * modes, width), BF16),
            pltpu.VMEM((2, pieces, half, rows // pieces, width), BF16),
            pltpu.VMEM((2, pieces, half, rows // pieces, width), BF16),
            pltpu.VMEM((2, pieces, half, rows // pieces, width), BF16),
            pltpu.VMEM((2, 2 * modes, width), BF16),
            pltpu.VMEM((2, rows, width), F32),
            pltpu.VMEM((rows, width), F32),
            pltpu.SemaphoreType.DMA,
        ]
        + [sems] * 8,
        compiler_params=pltpu.CompilerParams(
            collective_id=0, has_side_effects=True, vmem_limit_bytes=VMEM_BYTES
        ),
    )(cos_base, sin_base, series, cotangent, mix_weight)
    return activated, series_grad, weight_gradient(spectrum, grad, mix_weight.shape[2])


def solution(mesh):
    in_specs = (
        P(("groups", "tm"), "chan"),
        P(("groups", "tm"), "chan"),
        P(),
        P(None, "tm", None, "chan"),
    )
    out_specs = (
        P(("groups", "tm"), "chan"),
        P(("groups", "tm"), "chan"),
        P("groups", "tm", None, "chan"),
    )
    return jax.shard_map(body, mesh=mesh, in_specs=in_specs, out_specs=out_specs, check_vma=False)
```

```python
import functools
import math

import jax
import jax.numpy as jnp
from jax import lax
from jax.experimental import pallas as pl
from jax.experimental.pallas import tpu as pltpu
from jax.sharding import PartitionSpec as P

LANES = 128
FINE = 16
PIECE_MODES = 64
WG_MODES = 32
MODES_PER_STEP = 8
VMEM_BYTES = 56 * 1024 * 1024
F32 = jnp.float32
BF16 = jnp.bfloat16


def base_tables(mode_index, first_step, device_count, time_total):
    owned = mode_index.shape[0] // device_count
    depth = min(owned, PIECE_MODES)
    frequency = mode_index.reshape(-1, 1, depth)
    shape = (frequency.shape[0], 2, depth)
    frequency = jnp.broadcast_to(frequency, shape).reshape(1, -1)
    quarter = jnp.arange(2, dtype=jnp.int32).reshape(1, 2, 1) * (time_total // 4)
    quarter = jnp.broadcast_to(quarter, shape).reshape(1, -1)
    row = jnp.arange(32, dtype=jnp.int32)
    steps = jnp.where(row < FINE, row, (row - FINE) * FINE)
    steps = jnp.where(row == 24, first_step, steps)
    steps = jnp.where(row == 25, first_step + LANES, steps)
    steps = jnp.where(row == 26, LANES, steps)
    steps = jnp.where(row > 26, 0, steps)[:, None]
    low_term = frequency * (steps % 1024) % time_total
    high_term = frequency * (steps // 1024) % time_total * 1024 % time_total
    shift = jnp.where((row[:, None] == 24) | (row[:, None] == 25), quarter, 0)
    residue = (low_term + high_term + shift) % time_total
    angle = residue.astype(F32) * (2.0 * math.pi / time_total)
    return jnp.cos(angle), jnp.sin(angle)


def start_blocks(cos_ref, sin_ref, lanes):
    fine_cos, fine_sin = cos_ref[0:FINE, lanes], sin_ref[0:FINE, lanes]
    first, second = [], []
    for coarse in range(FINE, FINE + LANES // FINE):
        coarse_cos, coarse_sin = cos_ref[coarse : coarse + 1, lanes], sin_ref[coarse : coarse + 1, lanes]
        step_cos = coarse_cos * fine_cos - coarse_sin * fine_sin
        step_sin = coarse_sin * fine_cos + coarse_cos * fine_sin
        first.append(cos_ref[24:25, lanes] * step_cos - sin_ref[24:25, lanes] * step_sin)
        second.append(cos_ref[25:26, lanes] * step_cos - sin_ref[25:26, lanes] * step_sin)
    turn = 2.0 * cos_ref[26:27, lanes]
    turn = jnp.broadcast_to(turn, (LANES, LANES))
    return jnp.concatenate(first, axis=0), jnp.concatenate(second, axis=0), turn


def lane_block(index):
    return pl.ds(pl.multiple_of(index * LANES, LANES), LANES)


def fill_tables(cos_ref, sin_ref, table, table_t):
    step_blocks = (table if table is not None else table_t).shape[0 if table is not None else 1] // LANES

    def chunk(index, carry):
        lanes = lane_block(index)
        before, now, turn = start_blocks(cos_ref, sin_ref, lanes)
        if table is None:
            before, now, turn = before.T, now.T, turn.T
        for block in range(step_blocks):
            place = slice(block * LANES, (block + 1) * LANES)
            if table is None:
                table_t[lanes, place] = before.astype(BF16)
            else:
                table[place, lanes] = before.astype(BF16)
            before, now = now, turn * now - before
        return carry

    lax.fori_loop(0, cos_ref.shape[1] // LANES, chunk, 0)


def block_masks(block_size, width):
    row = lax.broadcasted_iota(jnp.int32, (block_size, width), 0)
    column = lax.broadcasted_iota(jnp.int32, (block_size, width), 1)
    pick = lax.rem(column, block_size) == row
    left = lax.div(lax.broadcasted_iota(jnp.int32, (width, width), 0), block_size)
    right = lax.div(lax.broadcasted_iota(jnp.int32, (width, width), 1), block_size)
    return pick, (left == right).astype(F32).astype(BF16)


def spread_rows(ref, first_row, block_size):
    rows = [
        jnp.broadcast_to(ref[pl.ds(first_row + k, 1), :], (block_size, ref.shape[1]))
        for k in range(MODES_PER_STEP)
    ]
    return jnp.concatenate(rows, axis=0)


def expand(ref, first_row, pick, same_block):
    rows = spread_rows(ref, first_row, pick.shape[0])
    rows = jnp.where(jnp.concatenate([pick] * MODES_PER_STEP, axis=0), rows, 0.0).astype(BF16)
    return jnp.dot(rows, same_block, preferred_element_type=F32)


def fold(values, block_size):
    return values.reshape(MODES_PER_STEP, block_size, values.shape[1]).sum(axis=1)


def loop(begin, end, step):
    if end - begin <= 8:
        for k in range(begin, end):
            step(k)
    else:

        def one(k, carry):
            step(k)
            return carry

        lax.fori_loop(begin, end, one, 0)


def mode_weights(weight, part, first_row):
    rows = weight[part, pl.ds(first_row, MODES_PER_STEP)]
    return rows.reshape(rows.shape[0] * rows.shape[1], rows.shape[2]).astype(F32)


def spectral_kernel(
    scale_in,
    scale_out,
    count,
    cos_ref,
    sin_ref,
    series,
    cotangent,
    weight_hbm,
    activated,
    series_grad,
    spectrum_out,
    grad_out,
    weight,
    table,
    table_t,
    field,
    grad_pre,
    grad_low,
    partial,
    pair_in,
    pair_sum,
    line_in,
    gathered,
    spectrum,
    rows_out,
    weight_sem,
    pair_send,
    pair_recv,
    line_send,
    line_recv,
    share_send,
    share_recv,
    cross_send,
    cross_recv,
):
    half = count // 2
    owned = weight.shape[1]
    block_size = weight.shape[2]
    rows = 2 * owned
    depth = min(owned, PIECE_MODES)
    pieces = owned // depth
    piece_rows = 2 * depth
    time_rows, width = series.shape
    me = lax.axis_index("tm")
    high, low = lax.div(me, 2), lax.rem(me, 2)
    partner = high * 2 + 1 - low

    def peer(offset):
        return lax.rem(high + offset, half) * 2 + low

    def offset_of(k):
        if half != 4:
            return k + 1
        return (2, 1, 3, 4)[k]

    def piece(device, q):
        return pl.ds(pl.multiple_of(device * rows + q * piece_rows, piece_rows), piece_rows)

    def block(device):
        return pl.ds(pl.multiple_of(device * rows, rows), rows)

    def copy(source, target, send_sem, recv_sem, device):
        return pltpu.make_async_remote_copy(
            src_ref=source,
            dst_ref=target,
            send_sem=send_sem,
            recv_sem=recv_sem,
            device_id={"tm": device},
            device_id_type=pl.DeviceIdType.MESH,
        )

    load = pltpu.make_async_copy(weight_hbm, weight, weight_sem)
    load.start()
    barrier = pltpu.get_barrier_semaphore()
    pl.semaphore_signal(barrier, inc=1, device_id={"tm": partner}, device_id_type=pl.DeviceIdType.MESH)

    def greet(offset, carry):
        pl.semaphore_signal(barrier, inc=1, device_id={"tm": peer(offset)}, device_id_type=pl.DeviceIdType.MESH)
        return carry

    lax.fori_loop(1, half, greet, 0)

    def pair_target(k):
        return lax.rem(high + offset_of(k), half) * 2 + 1 - low

    def pair_copy(phase, q, k):
        return copy(
            partial.at[phase, piece(pair_target(k), q)],
            pair_in.at[phase, q, k],
            pair_send.at[phase, q, k],
            pair_recv.at[phase, q, k],
            partner,
        )

    def line_copy(phase, q, k):
        return copy(
            pair_sum.at[phase, q, k],
            line_in.at[phase, q, k],
            line_send.at[phase, q, k],
            line_recv.at[phase, q, k],
            peer(offset_of(k)),
        )

    def share_copy(phase, q, k):
        mine = gathered.at[phase, piece(me, q)]
        return copy(mine, mine, share_send.at[phase, q, k], share_recv.at[phase, q, k], peer(k))

    def cross_copy(phase, q, k):
        held = gathered.at[phase, piece(lax.rem(high - k + half, half) * 2 + low, q)]
        return copy(held, held, cross_send.at[phase, q, k], cross_recv.at[phase, q, k], partner)

    def arrival(phase, device, q, recv_sem):
        place = gathered.at[phase, piece(device, q)]
        return copy(place, place, recv_sem, recv_sem, partner)

    def exchange(phase, signal, factor, mode_step, meanwhile):
        def project(device):
            product = jnp.dot(table_t[block(device), :], signal[...], preferred_element_type=F32)
            partial[phase, block(device), :] = (product * factor).astype(BF16)

        def send_first(k):
            project(pair_target(k))
            pair_copy(phase, 0, k).start()

        def forward(q):
            def one(k):
                device = lax.rem(high - k + half, half) * 2 + low
                arrival(phase, device, q, share_recv.at[phase, q, k]).wait_recv()
                cross_copy(phase, q, k).start()

            loop(1, half, one)

        def line_piece(q):
            def send_line(k):
                pair_copy(phase, q, k).wait_recv()
                own = partial[phase, piece(peer(offset_of(k)), q), :].astype(F32)
                pair_sum[phase, q, k] = (own + pair_in[phase, q, k].astype(F32)).astype(BF16)
                line_copy(phase, q, k).start()

            loop(0, half - 1, send_line)

        def mix_piece(q):
            place = pl.ds(q * piece_rows, piece_rows)
            pair_copy(phase, q, half - 1).wait_recv()
            spectrum[phase, place, :] = (
                partial[phase, piece(me, q), :].astype(F32) + pair_in[phase, q, half - 1].astype(F32)
            )

            def add(k):
                line_copy(phase, q, k).wait_recv()
                spectrum[phase, place, :] += line_in[phase, q, k].astype(F32)

            loop(0, half - 1, add)
            spectrum[phase, place, :] = spectrum[phase, place, :].astype(BF16).astype(F32)
            if phase == 0 and q == 0:
                load.wait()

            def mode_steps(step, carry):
                first = pl.multiple_of(q * piece_rows + step * MODES_PER_STEP, MODES_PER_STEP)
                mode_step(first, first + depth, pl.multiple_of(q * depth + step * MODES_PER_STEP, MODES_PER_STEP))
                return carry

            lax.fori_loop(0, depth // MODES_PER_STEP, mode_steps, 0)
            gathered[phase, piece(me, q), :] = rows_out[place, :].astype(BF16)
            loop(1, half, lambda k: share_copy(phase, q, k).start())
            cross_copy(phase, q, 0).start()

        loop(0, half, send_first)
        for q in range(1, pieces):
            loop(0, half, lambda k: pair_copy(phase, q, k).start())
        loop(0, half, lambda k: project(peer(offset_of(k))))
        for q in range(pieces):
            line_piece(q)
            if q == 0:
                meanwhile()
            if q > 0:
                mix_piece(q - 1)
            if q > 1:
                forward(q - 2)
        mix_piece(pieces - 1)
        if pieces > 1:
            forward(pieces - 2)
        early = rows % LANES == 0
        if early:
            add_block(phase, me * rows, rows, True)
        forward(pieces - 1)
        if early:
            loop(1, half, lambda k: add_block(phase, (lax.rem(high - k + half, half) * 2 + low) * rows, rows, False))

        def receive(k):
            device = lax.rem(high - k + half, half) * 2 + 1 - low
            for q in range(pieces):
                arrival(phase, device, q, cross_recv.at[phase, q, k]).wait_recv()
            if early:
                add_block(phase, device * rows, rows, False)

        loop(0, half, receive)
        if not early:
            add_block(phase, 0, 2 * LANES, True)
            loop(1, count * rows // (2 * LANES), lambda u: add_block(phase, u * 2 * LANES, 2 * LANES, False))

        def sent(k):
            for q in range(pieces):
                pair_copy(phase, q, k).wait_send()
                cross_copy(phase, q, k).wait_send()

        def sent_line(k):
            for q in range(pieces):
                line_copy(phase, q, k).wait_send()
                share_copy(phase, q, k + 1).wait_send()

        loop(0, half, sent)
        loop(0, half - 1, sent_line)

    def add_block(phase, first_row, depth, begin):
        place = pl.ds(pl.multiple_of(first_row, depth), depth)
        right = gathered[phase, place, :]

        def tile(t, carry):
            steps = pl.ds(pl.multiple_of(t * 2 * LANES, 2 * LANES), 2 * LANES)
            product = jnp.dot(table[steps, place], right, preferred_element_type=F32)
            if begin:
                field[steps, :] = product
            else:
                field[steps, :] += product
            return carry

        lax.fori_loop(0, time_rows // (2 * LANES), tile, 0)

    pick, same_block = block_masks(block_size, width)

    def mix(first, second, mode):
        x_real = expand(spectrum.at[0], first, pick, same_block)
        x_imag = expand(spectrum.at[0], second, pick, same_block)
        w_real, w_imag = mode_weights(weight, 0, mode), mode_weights(weight, 1, mode)
        rows_out[pl.ds(first, MODES_PER_STEP), :] = fold(x_real * w_real - x_imag * w_imag, block_size)
        rows_out[pl.ds(second, MODES_PER_STEP), :] = fold(x_real * w_imag + x_imag * w_real, block_size)

    def mix_back(first, second, mode):
        g_real = spread_rows(spectrum.at[1], first, block_size)
        g_imag = spread_rows(spectrum.at[1], second, block_size)
        w_real, w_imag = mode_weights(weight, 0, mode), mode_weights(weight, 1, mode)
        chosen = jnp.concatenate([pick] * MODES_PER_STEP, axis=0)

        def gathered_rows(values):
            sums = jnp.dot(values.astype(BF16), same_block, preferred_element_type=F32)
            return fold(jnp.where(chosen, sums, 0.0), block_size)

        rows_out[pl.ds(first, MODES_PER_STEP), :] = gathered_rows(w_real * g_real + w_imag * g_imag)
        rows_out[pl.ds(second, MODES_PER_STEP), :] = gathered_rows(w_real * g_imag - w_imag * g_real)

    fill_tables(cos_ref, sin_ref, None, table_t)
    pl.semaphore_wait(barrier, half)
    exchange(0, series, scale_in, mix, lambda: fill_tables(cos_ref, sin_ref, table, None))

    slope = math.sqrt(2.0 / math.pi)

    def activate(t, carry):
        steps = pl.ds(pl.multiple_of(t * LANES, LANES), LANES)
        value = series[steps, :].astype(F32) + scale_out * field[steps, :]
        square = value * value
        tanh = jnp.tanh(slope * (value + 0.044715 * (square * value)))
        gate = 0.5 * (1.0 + tanh)
        activated[steps, :] = (value * gate).astype(BF16)
        inner = slope * (1.0 + 3.0 * 0.044715 * square)
        derivative = gate + 0.5 * value * (1.0 - tanh * tanh) * inner
        grad = cotangent[steps, :].astype(F32) * derivative
        grad_pre[steps, :] = grad
        grad_low[steps, :] = grad.astype(BF16)
        return carry

    lax.fori_loop(0, time_rows // LANES, activate, 0)
    exchange(1, grad_low, scale_out, mix_back, lambda: None)
    spectrum_out[...] = spectrum[0]
    grad_out[...] = spectrum[1]

    def finish(t, carry):
        steps = pl.ds(pl.multiple_of(t * LANES, LANES), LANES)
        series_grad[steps, :] = (grad_pre[steps, :] + scale_in * field[steps, :]).astype(BF16)
        return carry

    lax.fori_loop(0, time_rows // LANES, finish, 0)


def weight_grad_kernel(x_real, x_imag, g_real, g_imag, out, pick_ref, same_ref):
    block_size, width = out.shape[2], out.shape[3]

    @pl.when(pl.program_id(0) == 0)
    def _():
        pick, same_block = block_masks(block_size, width)
        pick_ref[...] = pick.astype(F32)
        same_ref[...] = same_block

    pick, same_block = pick_ref[...] > 0.5, same_ref[...]
    spread = jnp.where(pick, 1.0, 0.0)

    for mode in range(out.shape[1]):
        row = slice(mode, mode + 1)
        gr, gi = g_real[row, :], g_imag[row, :]
        xr = jnp.dot((spread * x_real[row, :]).astype(BF16), same_block, preferred_element_type=F32)
        xi = jnp.dot((spread * x_imag[row, :]).astype(BF16), same_block, preferred_element_type=F32)
        out[0, mode] = xr * gr + xi * gi
        out[1, mode] = xr * gi - xi * gr


def weight_gradient(spectrum, grad, block_size):
    owned, width = spectrum.shape[0] // 2, spectrum.shape[1]
    step_modes = min(owned, WG_MODES)
    steps = owned // step_modes
    per_piece = min(owned, PIECE_MODES) // step_modes

    def place(part):
        return lambda g: (g // per_piece * (2 * per_piece) + part * per_piece + g % per_piece, 0)

    real = pl.BlockSpec((step_modes, width), place(0))
    imag = pl.BlockSpec((step_modes, width), place(1))
    return pl.pallas_call(
        weight_grad_kernel,
        grid=(steps,),
        in_specs=[real, imag, real, imag],
        out_specs=pl.BlockSpec((2, step_modes, block_size, width), lambda g: (0, g, 0, 0)),
        out_shape=jax.ShapeDtypeStruct((2, owned, block_size, width), F32),
        scratch_shapes=[pltpu.VMEM((block_size, width), F32), pltpu.VMEM((width, width), BF16)],
        compiler_params=pltpu.CompilerParams(vmem_limit_bytes=VMEM_BYTES),
    )(spectrum, spectrum, grad, grad)


def body(series, cotangent, mode_index, mix_weight):
    time_rows, width = series.shape
    count = lax.axis_size("tm")
    modes = mode_index.shape[0]
    owned = mix_weight.shape[1]
    rows = 2 * owned
    half = count // 2
    pieces = max(1, owned // PIECE_MODES)
    time_total = time_rows * count
    cos_base, sin_base = base_tables(mode_index, lax.axis_index("tm") * time_rows, count, time_total)
    kernel = functools.partial(
        spectral_kernel, 1.0 / math.sqrt(time_total), math.sqrt(2.0 / modes), count
    )
    vmem = pl.BlockSpec(memory_space=pltpu.VMEM)
    sems = pltpu.SemaphoreType.DMA((2, pieces, half))
    activated, series_grad, spectrum, grad = pl.pallas_call(
        kernel,
        in_specs=[vmem] * 4 + [pl.BlockSpec(memory_space=pl.ANY)],
        out_specs=[vmem] * 4,
        out_shape=[
            jax.ShapeDtypeStruct((time_rows, width), BF16),
            jax.ShapeDtypeStruct((time_rows, width), BF16),
            jax.ShapeDtypeStruct((rows, width), F32),
            jax.ShapeDtypeStruct((rows, width), F32),
        ],
        scratch_shapes=[
            pltpu.VMEM(mix_weight.shape, BF16),
            pltpu.VMEM((time_rows, 2 * modes), BF16),
            pltpu.VMEM((2 * modes, time_rows), BF16),
            pltpu.VMEM((time_rows, width), F32),
            pltpu.VMEM((time_rows, width), F32),
            pltpu.VMEM((time_rows, width), BF16),
            pltpu.VMEM((2, 2 * modes, width), BF16),
            pltpu.VMEM((2, pieces, half, rows // pieces, width), BF16),
            pltpu.VMEM((2, pieces, half, rows // pieces, width), BF16),
            pltpu.VMEM((2, pieces, half, rows // pieces, width), BF16),
            pltpu.VMEM((2, 2 * modes, width), BF16),
            pltpu.VMEM((2, rows, width), F32),
            pltpu.VMEM((rows, width), F32),
            pltpu.SemaphoreType.DMA,
        ]
        + [sems] * 8,
        compiler_params=pltpu.CompilerParams(
            collective_id=0, has_side_effects=True, vmem_limit_bytes=VMEM_BYTES
        ),
    )(cos_base, sin_base, series, cotangent, mix_weight)
    return activated, series_grad, weight_gradient(spectrum, grad, mix_weight.shape[2])


def solution(mesh):
    in_specs = (
        P(("groups", "tm"), "chan"),
        P(("groups", "tm"), "chan"),
        P(),
        P(None, "tm", None, "chan"),
    )
    out_specs = (
        P(("groups", "tm"), "chan"),
        P(("groups", "tm"), "chan"),
        P("groups", "tm", None, "chan"),
    )
    return jax.shard_map(body, mesh=mesh, in_specs=in_specs, out_specs=out_specs, check_vma=False)
```
